32 devices in a mesh: group: 2 (over x), tm: 16 (over z, y, core).
Axes of the slice: x: 2, y: 2, z: 4, core: 2. Of those that a mesh axis runs over, the one named last changes fastest.
Arguments:
- patches: bfloat16 [32, 1024, 128], P(('group', 'tm')), parts along dimension 0, may hold values from -6 to 6
- classes: int32 [32], P(('group', 'tm')), parts along dimension 0, may hold values from 0 to 15
- dilations: int32 [4], replicated, may hold values from 1 to 4, as said below
- enc_weight: bfloat16 [128, 256], replicated, may hold values from -0.5 to 0.5
- cond_table: bfloat16 [16, 256], replicated, may hold values from -3 to 3
- temp_weight: bfloat16 [4, 512, 256], replicated, may hold values from -0.25 to 0.25
- dec_weight: bfloat16 [256, 128], replicated, may hold values from -0.375 to 0.375
- cotangent: bfloat16 [32, 1024, 128], P(('group', 'tm')), parts along dimension 0, may hold values from -0.125 to 0.125
Outputs:
- decoded: bfloat16 [32, 1024, 128], P(('group', 'tm')), parts along dimension 0
- grad_encoder: float32 [256, 256], P(('group', 'tm')), parts along dimension 0
- grad_temporal: float32 [8, 512, 256], P('group', 'tm'), parts along dimension 0
- grad_decoder: float32 [512, 128], P(('group', 'tm')), parts along dimension 0
The draws below stay inside these ranges and needn't reach their ends.
There are 2 independent parts, one for each index of `group`. The reference program is written for one: setup_inputs(seed, part) draws one part's arguments, and reference() takes and returns one part's arrays. A program takes and returns all parts, laid end to end along the dimension named above; an argument that names none is the same for every part. Nothing has to cross between parts.
Inputs may be any that keep to these rules, and one draw needn't show every extreme that they name: `dilations`: every layer's dilation lies in 1 to 4, and some layer's is exactly 4.
All inputs are finite; a program needn't handle non-finite values.
Results may differ from the reference program's by a relative error of at most 0.009.
Values may be sent and summed in bfloat16 or wider, within the bound.
A program may use at most 64 MiB of HBM per device.

```python
import jax
import jax.numpy as jnp
from jax import lax

LAT = 256
PF = 128
NCLS = 16
LAYERS = 4
LPIX = 1024
T_SIZE = 16
DMAX = 4


def draw_dilations(key, part):
    first_key, second_key = jax.random.split(jax.random.fold_in(key, 17))
    spacing = jax.random.randint(first_key, (LAYERS,), 1, DMAX + 1)
    chosen = jax.random.randint(second_key, (), 0, LAYERS)
    return jnp.where(jnp.arange(LAYERS) == chosen, DMAX, spacing).astype(jnp.int32)


def plant(array, own_key, low, high):
    longest = array.shape.index(max(array.shape))
    spots = []
    for shift in (0, 1):
        where = [jax.random.randint(jax.random.fold_in(own_key, axis), (), 0, length) for axis, length in enumerate(array.shape)]
        where[longest] = (where[longest] + shift) % array.shape[longest]
        spots.append(tuple(where))
    return array.at[spots[0]].set(low).at[spots[1]].set(high)


def shard_levels(own_key, extent, cuts, low, high):
    level, own = 1.0, jax.random.fold_in(own_key, 6)
    for dim, parts in cuts:
        draws = jnp.exp(jax.random.uniform(jax.random.fold_in(own, dim), (parts,), jnp.float32, low / len(cuts), high / len(cuts)))
        level = level * jnp.repeat(draws, extent[dim] // parts).reshape([-1 if axis == dim else 1 for axis in range(len(extent))])
    return level


def gaussian(key, shape, scale, reach, pieces=(), kind=jnp.bfloat16):
    drawn = scale * jax.random.normal(key, shape, jnp.float32)
    if pieces:
        drawn = drawn * shard_levels(key, shape, pieces, -0.22, 0.18)
    return jnp.clip(drawn, -reach, reach).astype(kind)


def setup_inputs(seed: int = 0, part: int = 0) -> dict:
    keys = jax.random.split(jax.random.key(seed), 9)
    own_keys = jax.random.split(jax.random.fold_in(keys[8], part), 9)
    patches = gaussian(own_keys[0], (T_SIZE, LPIX, PF), 1.0, 6.0, ((0, 16),))
    classes = plant(jax.random.randint(own_keys[1], (T_SIZE,), 0, NCLS), jax.random.fold_in(own_keys[1], 1), 0, NCLS - 1).astype(jnp.int32)
    dilations = draw_dilations(jax.random.fold_in(keys[8], 71), part)
    enc_weight = gaussian(keys[3], (PF, LAT), PF ** -0.5, 0.5)
    cond_table = gaussian(keys[4], (NCLS, LAT), 0.5, 3.0)
    temp_weight = gaussian(keys[5], (LAYERS, 2 * LAT, LAT), (2 * LAT) ** -0.5, 0.25)
    dec_weight = gaussian(keys[6], (LAT, PF), LAT ** -0.5, 0.375)
    cotangent = gaussian(own_keys[7], (T_SIZE, LPIX, PF), ((T_SIZE * LPIX) ** -0.5), 0.125, ((0, 16),))
    return dict(patches=patches, classes=classes, dilations=dilations, enc_weight=enc_weight, cond_table=cond_table, temp_weight=temp_weight, dec_weight=dec_weight, cotangent=cotangent)


def reference(patches, classes, dilations, enc_weight, cond_table, temp_weight, dec_weight, cotangent):
    frame_count, pixel_count, feature_count = patches.shape
    block_count = pixel_count // 128
    embedded = cond_table.astype(jnp.float32)[classes]
    positions = jnp.arange(frame_count)

    def shift_late(values, spacing):
        moved = jnp.roll(values, spacing, axis=0)
        return jnp.where((positions >= spacing)[:, None, None], moved, jnp.zeros_like(moved))

    def shift_early(values, spacing):
        moved = jnp.roll(values, -spacing, axis=0)
        return jnp.where((positions < frame_count - spacing)[:, None, None], moved, jnp.zeros_like(moved))

    def one_block(carry, inputs):
        enc_sum, temp_sum, dec_sum = carry
        patch_block, cot_block = inputs
        start = jnp.einsum('tpc,cd->tpd', patch_block.astype(jnp.float32), enc_weight.astype(jnp.float32))
        latent = (start + embedded[:, None, :]).astype(jnp.bfloat16)
        saved = []
        for layer in range(LAYERS):
            joined = jnp.concatenate([latent, shift_late(latent, dilations[layer])], axis=-1)
            pre_act = jnp.einsum('tpk,kd->tpd', joined.astype(jnp.float32), temp_weight[layer].astype(jnp.float32))
            saved.append((joined, pre_act))
            latent = (latent.astype(jnp.float32) + jax.nn.silu(pre_act)).astype(jnp.bfloat16)
        decoded = jnp.einsum('tpd,dc->tpc', latent.astype(jnp.float32), dec_weight.astype(jnp.float32)).astype(jnp.bfloat16)
        dec_term = jnp.einsum('tpd,tpc->dc', latent.astype(jnp.float32), cot_block.astype(jnp.float32))
        carried = jnp.einsum('tpc,dc->tpd', cot_block.astype(jnp.float32), dec_weight.astype(jnp.float32)).astype(jnp.bfloat16)
        layer_terms = [None] * LAYERS
        for layer in reversed(range(LAYERS)):
            joined, pre_act = saved[layer]
            gate_value = jax.nn.sigmoid(pre_act)
            dpre = (carried.astype(jnp.float32) * gate_value * (1.0 + pre_act * (1.0 - gate_value))).astype(jnp.bfloat16)
            layer_terms[layer] = jnp.einsum('tpk,tpd->kd', joined.astype(jnp.float32), dpre.astype(jnp.float32))
            returned = jnp.einsum('tpd,kd->tpk', dpre.astype(jnp.float32), temp_weight[layer].astype(jnp.float32))
            carried = (carried.astype(jnp.float32) + returned[..., :LAT] + shift_early(returned[..., LAT:], dilations[layer])).astype(jnp.bfloat16)
        enc_term = jnp.einsum('tpc,tpd->cd', patch_block.astype(jnp.float32), carried.astype(jnp.float32))
        return (enc_sum + enc_term, temp_sum + jnp.stack(layer_terms), dec_sum + dec_term), decoded

    patch_blocks = patches.reshape(frame_count, block_count, 128, feature_count).transpose(1, 0, 2, 3)
    cot_blocks = cotangent.reshape(frame_count, block_count, 128, feature_count).transpose(1, 0, 2, 3)
    init = (jnp.zeros((PF, LAT), jnp.float32), jnp.zeros((LAYERS, 2 * LAT, LAT), jnp.float32), jnp.zeros((LAT, PF), jnp.float32))
    sums, decoded_blocks = lax.scan(one_block, init, (patch_blocks, cot_blocks))
    decoded = decoded_blocks.transpose(1, 0, 2, 3).reshape(frame_count, pixel_count, feature_count)
    return (decoded, sums[0], sums[1], sums[2])
```

```python
import functools

import jax
import jax.numpy as jnp
from jax import lax
from jax.experimental import pallas as pl
from jax.experimental.pallas import tpu as pltpu
from jax.sharding import PartitionSpec as P

MESH = pl.DeviceIdType.MESH
F32 = jnp.float32
BF16 = jnp.bfloat16

PATCH, EMBED, COTAN, DECODE, SMALL, LAYER = 0, 1, 2, 3, 4, 5


def dot_nt(a, b):
    return lax.dot_general(a, b, (((1,), (1,)), ((), ())), preferred_element_type=F32)


def dot_nn(a, b):
    return jnp.dot(a, b, preferred_element_type=F32)


def step_kernel(
    n, layers, margin, chunk,
    dil, kind_row, patches, enc_w, temp_w, dec_w, cot,
    decoded, grad_enc, grad_temp, grad_dec,
    px, ct, emb, lat, slope, lat_t, px_t, dpre, car, dec_send, g_send, g_recv, s_send, s_recv,
    send_sem, recv_sem,
):
    me = lax.axis_index("tm")
    block = px.shape[1]
    tokens = n * block
    width = enc_w.shape[1]
    spans = [(c * chunk, chunk) for c in range(tokens // chunk)]

    def latents(layer, lo, size):
        first = margin + lo // block
        return lat[layer, first : first + size // block].reshape(size, width)

    def put_latents(layer, lo, value):
        first = margin + lo // block
        frames = value.shape[0] // block
        lat[layer, first : first + frames] = value.reshape(frames, block, width)

    def late_latents(layer, lo, size):
        back = margin - dil[layer] + lo // block
        return jnp.concatenate([lat[layer, back + i] for i in range(size // block)], axis=0)

    def early_dpre(layer, lo, size):
        ahead = dil[layer] + lo // block
        return jnp.concatenate([dpre[ahead + i] for i in range(size // block)], axis=0)

    def copy(kind, k, src, dst):
        return pltpu.make_async_remote_copy(
            src_ref=src,
            dst_ref=dst,
            send_sem=send_sem.at[kind, k],
            recv_sem=recv_sem.at[kind, k],
            device_id={"tm": lax.rem(me + k, n)},
            device_id_type=MESH,
        )

    def descriptor(kind, k):
        peer = lax.rem(me + k, n)
        if kind == PATCH:
            return copy(kind, k, patches.at[peer], px.at[me])
        if kind == EMBED:
            return copy(kind, k, emb.at[me], emb.at[me])
        if kind == COTAN:
            return copy(kind, k, cot.at[peer], ct.at[me])
        if kind == DECODE:
            return copy(kind, k, dec_send.at[peer], decoded.at[me])
        if kind == SMALL:
            return copy(kind, k, s_send.at[peer], s_recv.at[k])
        return copy(kind, k, g_send.at[kind - LAYER, peer], g_recv.at[kind - LAYER, k])

    def landing(kind, k):
        source = lax.rem(me + n - k, n)
        if kind == PATCH:
            return copy(kind, k, patches.at[me], px.at[source])
        if kind == EMBED:
            return copy(kind, k, emb.at[me], emb.at[source])
        if kind == COTAN:
            return copy(kind, k, cot.at[me], ct.at[source])
        if kind == DECODE:
            return copy(kind, k, dec_send.at[me], decoded.at[source])
        return descriptor(kind, k)

    def each(fn):
        lax.fori_loop(1, n, lambda k, c: (fn(k), c)[1], 0)

    def start(kind):
        each(lambda k: descriptor(kind, k).start())

    def arrive(kind):
        each(lambda k: landing(kind, k).wait_recv())

    def sent(kind):
        each(lambda k: descriptor(kind, k).wait_send())

    barrier = pltpu.get_barrier_semaphore()
    each(
        lambda k: pl.semaphore_signal(
            barrier, inc=1, device_id={"tm": lax.rem(me + k, n)}, device_id_type=MESH
        )
    )
    emb[me] = kind_row[...]
    pl.semaphore_wait(barrier, n - 1)
    start(PATCH)
    start(EMBED)

    px[me] = patches[me]
    ct[me] = cot[me]
    for layer in range(layers):
        lat[layer, 0:margin] = jnp.zeros((margin, block, width), BF16)
    dpre[n : n + margin] = jnp.zeros((margin, block, width), BF16)

    arrive(PATCH)
    arrive(EMBED)
    start(COTAN)

    for lo, size in spans:
        frames = size // block
        first = lo // block
        rows = px[first : first + frames].reshape(size, px.shape[2])
        begin = dot_nn(rows, enc_w[...]).reshape(frames, block, width)
        begin = begin + emb[first : first + frames]
        put_latents(0, lo, begin.reshape(size, width).astype(BF16))
        px_t[:, lo : lo + size] = rows.T

    for layer in range(layers):
        for lo, size in spans:
            now = latents(layer, lo, size)
            late = late_latents(layer, lo, size)
            pre = dot_nn(now, temp_w[layer, 0:width, :]) + dot_nn(late, temp_w[layer, width:, :])
            s = 0.5 + 0.5 * jnp.tanh(0.5 * pre)
            act = pre * s
            put_latents(layer + 1, lo, (now.astype(F32) + act).astype(BF16))
            slope[layer, lo : lo + size, :] = s + act * (1.0 - s)
            lat_t[layer, :, lo : lo + size] = now.T

    for lo, size in spans:
        now = latents(layers, lo, size)
        out = dot_nn(now, dec_w[...]).astype(BF16)
        dec_send[lo // block : (lo + size) // block] = out.reshape(size // block, block, out.shape[1])
        lat_t[layers, :, lo : lo + size] = now.T
    start(DECODE)
    decoded[me] = dec_send[me]
    arrive(COTAN)

    for lo, size in spans:
        rows = ct[lo // block : (lo + size) // block].reshape(size, ct.shape[2])
        car[lo : lo + size, :] = dot_nt(rows, dec_w[...]).astype(BF16)

    dec_rows = s_send.shape[1] // 2
    whole_ct = ct[...].reshape(tokens, ct.shape[2])
    dec_term = dot_nn(lat_t[layers], whole_ct).astype(BF16)
    s_send[:, 0:dec_rows, :] = dec_term.reshape(n, dec_rows, dec_term.shape[1])

    for layer in reversed(range(layers)):
        for lo, size in spans:
            product = car[lo : lo + size, :].astype(F32) * slope[layer, lo : lo + size, :]
            dpre[lo // block : (lo + size) // block] = product.astype(BF16).reshape(
                size // block, block, width
            )
        half = n // 2
        top = dot_nn(lat_t[layer], dpre[0:n].reshape(tokens, width))
        g_send[layer, 0:half] = top.astype(BF16).reshape(half, width // half, width)
        low = dot_nn(lat_t[layer], early_dpre(layer, 0, tokens))
        g_send[layer, half:n] = low.astype(BF16).reshape(half, width // half, width)
        start(LAYER + layer)
        for lo, size in spans:
            same = dpre[lo // block : (lo + size) // block].reshape(size, width)
            back = dot_nt(same, temp_w[layer, 0:width, :])
            back = back + dot_nt(early_dpre(layer, lo, size), temp_w[layer, width:, :])
            car[lo : lo + size, :] = (car[lo : lo + size, :].astype(F32) + back).astype(BF16)

    enc_term = dot_nn(px_t[...], car[...])
    enc_term = enc_term.reshape(n, enc_term.shape[0] // n, width)
    lanes = s_send.shape[2]
    enc_term = jnp.concatenate(
        [enc_term[:, :, i : i + lanes] for i in range(0, width, lanes)], axis=1
    )
    s_send[:, dec_rows:, :] = enc_term.astype(BF16)
    start(SMALL)

    for layer in reversed(range(layers)):
        arrive(LAYER + layer)
        total = g_send[layer, me].astype(F32)
        for k in range(1, n):
            total = total + g_recv[layer, k].astype(F32)
        grad_temp[layer] = total
    arrive(SMALL)
    total = s_send[me].astype(F32)
    for k in range(1, n):
        total = total + s_recv[k].astype(F32)
    grad_dec[...] = total[0:dec_rows]
    enc_rows = grad_enc.shape[0]
    for i in range(width // lanes):
        first = dec_rows + i * enc_rows
        grad_enc[:, i * lanes : (i + 1) * lanes] = total[first : first + enc_rows]
    arrive(DECODE)
    for kind in range(LAYER + layers):
        sent(kind)


def kernel_shards(
    n, patches, classes, dilations, enc_weight, cond_table, temp_weight, dec_weight, cotangent
):
    _, pixels, features = patches.shape
    layers, deep, width = temp_weight.shape
    block = pixels // n
    margin = n // 4
    tokens = n * block
    own = deep // n
    lanes = features
    small = 2 * (width // n)
    vmem = pl.BlockSpec(memory_space=pltpu.VMEM)
    smem = pl.BlockSpec(memory_space=pltpu.SMEM)
    chunk = tokens // 2
    kinds = cond_table.shape[0]
    onehot = (classes[:, None] == jnp.arange(kinds, dtype=jnp.int32)[None, :]).astype(BF16)
    kind_row = jnp.dot(onehot, cond_table, preferred_element_type=F32)
    decoded, grad_enc, grad_temp, grad_dec = pl.pallas_call(
        functools.partial(step_kernel, n, layers, margin, chunk),
        out_shape=(
            jax.ShapeDtypeStruct((n, block, features), BF16),
            jax.ShapeDtypeStruct((features // n, width), F32),
            jax.ShapeDtypeStruct((layers, own, width), F32),
            jax.ShapeDtypeStruct((width // n, features), F32),
        ),
        in_specs=[smem] + [vmem] * 6,
        out_specs=(vmem,) * 4,
        scratch_shapes=[
            pltpu.VMEM((n, block, features), BF16),
            pltpu.VMEM((n, block, features), BF16),
            pltpu.VMEM((n, 1, width), F32),
            pltpu.VMEM((layers + 1, margin + n, block, width), BF16),
            pltpu.VMEM((layers, tokens, width), F32),
            pltpu.VMEM((layers + 1, width, tokens), BF16),
            pltpu.VMEM((features, tokens), BF16),
            pltpu.VMEM((n + margin, block, width), BF16),
            pltpu.VMEM((tokens, width), BF16),
            pltpu.VMEM((n, block, features), BF16),
            pltpu.VMEM((layers, n, own, width), BF16),
            pltpu.VMEM((layers, n, own, width), BF16),
            pltpu.VMEM((n, small, lanes), BF16),
            pltpu.VMEM((n, small, lanes), BF16),
            pltpu.SemaphoreType.DMA((LAYER + layers, n)),
            pltpu.SemaphoreType.DMA((LAYER + layers, n)),
        ],
        compiler_params=pltpu.CompilerParams(
            collective_id=0, has_side_effects=True, vmem_limit_bytes=48 * 1024 * 1024
        ),
    )(
        dilations, kind_row, patches.reshape(n, block, features), enc_weight,
        temp_weight, dec_weight, cotangent.reshape(n, block, features),
    )
    return decoded.reshape(1, pixels, features), grad_enc, grad_temp, grad_dec


def shift_late(values, spacing, margin):
    filler = jnp.zeros((margin,) + values.shape[1:], values.dtype)
    padded = jnp.concatenate([filler, values], axis=0)
    return lax.dynamic_slice_in_dim(padded, margin - spacing, values.shape[0], 0)


def shift_early(values, spacing, margin):
    filler = jnp.zeros((margin,) + values.shape[1:], values.dtype)
    padded = jnp.concatenate([values, filler], axis=0)
    return lax.dynamic_slice_in_dim(padded, spacing, values.shape[0], 0)


def plain_shards(
    patches, classes, dilations, enc_weight, cond_table, temp_weight, dec_weight, cotangent
):
    layers, _, width = temp_weight.shape
    block_patches = lax.all_to_all(patches, "tm", split_axis=1, concat_axis=0, tiled=True)
    block_cot = lax.all_to_all(cotangent, "tm", split_axis=1, concat_axis=0, tiled=True)
    frame_kinds = lax.all_gather(classes, "tm", tiled=True)
    kinds = cond_table.shape[0]
    onehot = (frame_kinds[:, None] == jnp.arange(kinds, dtype=jnp.int32)[None, :]).astype(BF16)
    embedded = jnp.dot(onehot, cond_table, preferred_element_type=F32)
    begin = jnp.einsum("tpc,cd->tpd", block_patches, enc_weight, preferred_element_type=F32)
    latent = (begin + embedded[:, None, :]).astype(BF16)
    margin = latent.shape[0] // 4
    saved = []
    for layer in range(layers):
        joined = jnp.concatenate([latent, shift_late(latent, dilations[layer], margin)], axis=-1)
        pre = jnp.einsum("tpk,kd->tpd", joined, temp_weight[layer], preferred_element_type=F32)
        saved.append((joined, pre))
        latent = (latent.astype(F32) + jax.nn.silu(pre)).astype(BF16)
    block_out = jnp.einsum(
        "tpd,dc->tpc", latent, dec_weight, preferred_element_type=F32
    ).astype(BF16)
    decoded = lax.all_to_all(block_out, "tm", split_axis=0, concat_axis=1, tiled=True)
    dec_term = jnp.einsum("tpd,tpc->dc", latent, block_cot, preferred_element_type=F32)
    carried = jnp.einsum(
        "tpc,dc->tpd", block_cot, dec_weight, preferred_element_type=F32
    ).astype(BF16)
    terms = [None] * layers
    for layer in reversed(range(layers)):
        joined, pre = saved[layer]
        s = jax.nn.sigmoid(pre)
        dpre = (carried.astype(F32) * s * (1.0 + pre * (1.0 - s))).astype(BF16)
        terms[layer] = jnp.einsum("tpk,tpd->kd", joined, dpre, preferred_element_type=F32)
        back = jnp.einsum("tpd,kd->tpk", dpre, temp_weight[layer], preferred_element_type=F32)
        carried = (
            carried.astype(F32)
            + back[..., :width]
            + shift_early(back[..., width:], dilations[layer], margin)
        ).astype(BF16)
    enc_term = jnp.einsum("tpc,tpd->cd", block_patches, carried, preferred_element_type=F32)
    return (
        decoded,
        lax.psum_scatter(enc_term, "tm", scatter_dimension=0, tiled=True),
        lax.psum_scatter(jnp.stack(terms), "tm", scatter_dimension=1, tiled=True),
        lax.psum_scatter(dec_term, "tm", scatter_dimension=0, tiled=True),
    )


def solution(mesh):
    n = mesh.shape["tm"]

    def shards(patches, *rest):
        pixels = patches.shape[1]
        deep, width = rest[4].shape[1:]
        whole = pixels % n == 0 and (pixels // n) % 16 == 0 and (deep // n) % 16 == 0
        if whole and patches.shape[0] == 1 and (width // n) % 16 == 0:
            return kernel_shards(n, patches, *rest)
        return plain_shards(patches, *rest)

    in_specs = (
        P(("group", "tm"), None, None),
        P(("group", "tm")),
        P(),
        P(),
        P(),
        P(),
        P(),
        P(("group", "tm"), None, None),
    )
    out_specs = (
        P(("group", "tm"), None, None),
        P(("group", "tm"), None),
        P("group", "tm", None),
        P(("group", "tm"), None),
    )
    return jax.shard_map(shards, mesh=mesh, in_specs=in_specs, out_specs=out_specs, check_vma=False)
```

```python
import functools

import jax
import jax.numpy as jnp
from jax import lax
from jax.experimental import pallas as pl
from jax.experimental.pallas import tpu as pltpu
from jax.sharding import PartitionSpec as P

MESH = pl.DeviceIdType.MESH
F32 = jnp.float32
BF16 = jnp.bfloat16

PATCH, EMBED, COTAN, DECODE, DEC_TERM, ENC_TERM = range(6)


def dot_nt(a, b):
    return lax.dot_general(a, b, (((1,), (1,)), ((), ())), preferred_element_type=F32)


def dot_nn(a, b):
    return jnp.dot(a, b, preferred_element_type=F32)


def step_kernel(
    n, layers, margin, chunk,
    dil, cls, patches, enc_hbm, cond_hbm, temp_hbm, dec_hbm, cot,
    decoded, grad_enc, grad_temp, grad_dec,
    enc_w, cond, temp_w, dec_w, cond_rows,
    px, ct, emb, lat, slope, lat_t, px_t, dpre, car, dec_send,
    core_out, core_in, y_out, y_in, z_out, z_in, d_out, d_in, e_out, e_in,
    local_sem, send_sem, recv_sem, stage_send, stage_recv,
):
    me = lax.axis_index("tm")
    core = lax.rem(me, 2)
    y = lax.rem(lax.div(me, 2), 2)
    z = lax.div(me, 4)
    nz = n // 4
    block = px.shape[1]
    tokens = n * block
    width = enc_w.shape[1]
    own = core_out.shape[4]

    local = [
        pltpu.make_async_copy(src, dst, local_sem.at[i])
        for i, (src, dst) in enumerate(
            [
                (cond_hbm, cond),
                (patches.at[me], px.at[me]),
                (enc_hbm, enc_w),
                (temp_hbm, temp_w),
                (dec_hbm, dec_w),
                (cot.at[me], ct.at[me]),
            ]
        )
    ]
    for fetch in local:
        fetch.start()

    def copy(kind, k, src, dst):
        return pltpu.make_async_remote_copy(
            src_ref=src,
            dst_ref=dst,
            send_sem=send_sem.at[kind, k],
            recv_sem=recv_sem.at[kind, k],
            device_id={"tm": lax.rem(me + k, n)},
            device_id_type=MESH,
        )

    def descriptor(kind, k):
        peer = lax.rem(me + k, n)
        if kind == PATCH:
            return copy(kind, k, patches.at[peer], px.at[me])
        if kind == EMBED:
            return copy(kind, k, emb.at[me], emb.at[me])
        if kind == COTAN:
            return copy(kind, k, cot.at[peer], ct.at[me])
        if kind == DECODE:
            return copy(kind, k, dec_send.at[peer], decoded.at[me])
        if kind == DEC_TERM:
            return copy(kind, k, d_out.at[peer], d_in.at[k])
        return copy(kind, k, e_out.at[peer], e_in.at[k])

    def landing(kind, k):
        source = lax.rem(me + n - k, n)
        if kind == PATCH:
            return copy(kind, k, patches.at[me], px.at[source])
        if kind == EMBED:
            return copy(kind, k, emb.at[me], emb.at[source])
        if kind == COTAN:
            return copy(kind, k, cot.at[me], ct.at[source])
        if kind == DECODE:
            return copy(kind, k, dec_send.at[me], decoded.at[source])
        return descriptor(kind, k)

    def each(fn):
        lax.fori_loop(1, n, lambda k, c: (fn(k), c)[1], 0)

    def start(kind):
        each(lambda k: descriptor(kind, k).start())

    def arrive(kind):
        each(lambda k: landing(kind, k).wait_recv())

    def sent(kind):
        each(lambda k: descriptor(kind, k).wait_send())

    def staged(layer, stage, src, dst, peer):
        return pltpu.make_async_remote_copy(
            src_ref=src,
            dst_ref=dst,
            send_sem=stage_send.at[layer, stage],
            recv_sem=stage_recv.at[layer, stage],
            device_id={"tm": peer},
            device_id_type=MESH,
        )

    def core_copy(layer):
        return staged(
            layer, 0, core_out.at[layer, 1 - core], core_in.at[layer], me + 1 - 2 * core
        )

    def y_copy(layer):
        return staged(layer, 1, y_out.at[layer], y_in.at[layer], me + 2 - 4 * y)

    def z_copy(layer, k):
        there = lax.rem(z + k, nz)
        peer = there * 4 + y * 2 + core
        return staged(layer, 1 + k, z_out.at[layer, there], z_in.at[layer, k], peer)

    def send_core(layer):
        core_copy(layer).start()

    def send_y(layer):
        core_copy(layer).wait_recv()
        total = core_out[layer, core, 1 - y].astype(F32) + core_in[layer, 1 - y].astype(F32)
        y_out[layer] = total.astype(BF16)
        y_copy(layer).start()

    def send_z(layer):
        y_copy(layer).wait_recv()
        total = core_out[layer, core, y].astype(F32) + core_in[layer, y].astype(F32)
        z_out[layer] = (total + y_in[layer].astype(F32)).astype(BF16)
        for k in range(1, nz):
            z_copy(layer, k).start()

    def finish(layer):
        total = z_out[layer, z].astype(F32)
        for k in range(1, nz):
            z_copy(layer, k).wait_recv()
            total = total + z_in[layer, k].astype(F32)
        grad_temp[layer] = total
        core_copy(layer).wait_send()
        y_copy(layer).wait_send()
        for k in range(1, nz):
            z_copy(layer, k).wait_send()

    barrier = pltpu.get_barrier_semaphore()
    each(
        lambda k: pl.semaphore_signal(
            barrier, inc=1, device_id={"tm": lax.rem(me + k, n)}, device_id_type=MESH
        )
    )
    pl.semaphore_wait(barrier, n - 1)
    start(PATCH)
    local[0].wait()
    kinds = cond.shape[0]
    cond_rows[...] = cond[...].astype(F32).reshape(kinds, 1, width)
    emb[me] = cond_rows[cls[0]]
    start(EMBED)

    spans = [(c * chunk, chunk) for c in range(tokens // chunk)]

    def latents(layer, lo, size):
        first = margin + lo // block
        return lat[layer, first : first + size // block].reshape(size, width)

    def put_latents(layer, lo, value):
        first = margin + lo // block
        frames = value.shape[0] // block
        lat[layer, first : first + frames] = value.reshape(frames, block, width)

    def late_latents(layer, lo, size):
        back = margin - dil[layer] + lo // block
        return jnp.concatenate([lat[layer, back + i] for i in range(size // block)], axis=0)

    def early_dpre(layer, lo, size):
        ahead = dil[layer] + lo // block
        return jnp.concatenate([dpre[ahead + i] for i in range(size // block)], axis=0)

    for layer in range(layers):
        lat[layer, 0:margin] = jnp.zeros((margin, block, width), BF16)
    dpre[n : n + margin] = jnp.zeros((margin, block, width), BF16)

    for fetch in local[1:]:
        fetch.wait()
    arrive(PATCH)
    start(COTAN)
    arrive(EMBED)

    for lo, size in spans:
        frames = size // block
        first = lo // block
        rows = px[first : first + frames].reshape(size, px.shape[2])
        begin = dot_nn(rows, enc_w[...]).reshape(frames, block, width)
        begin = begin + emb[first : first + frames]
        put_latents(0, lo, begin.reshape(size, width).astype(BF16))
        px_t[:, lo : lo + size] = rows.T

    for layer in range(layers):
        for lo, size in spans:
            now = latents(layer, lo, size)
            late = late_latents(layer, lo, size)
            pre = dot_nn(now, temp_w[layer, 0:width, :]) + dot_nn(late, temp_w[layer, width:, :])
            s = 0.5 + 0.5 * jnp.tanh(0.5 * pre)
            act = pre * s
            put_latents(layer + 1, lo, (now.astype(F32) + act).astype(BF16))
            slope[layer, lo : lo + size, :] = s + act * (1.0 - s)
            lat_t[layer, :, lo : lo + size] = now.T

    for lo, size in spans:
        now = latents(layers, lo, size)
        out = dot_nn(now, dec_w[...]).astype(BF16)
        dec_send[lo // block : (lo + size) // block] = out.reshape(size // block, block, out.shape[1])
        lat_t[layers, :, lo : lo + size] = now.T
    start(DECODE)
    decoded[me] = dec_send[me]
    arrive(COTAN)

    for lo, size in spans:
        rows = ct[lo // block : (lo + size) // block].reshape(size, ct.shape[2])
        car[lo : lo + size, :] = dot_nt(rows, dec_w[...]).astype(BF16)

    dec_rows = d_out.shape[1]
    whole_ct = ct[...].reshape(tokens, ct.shape[2])
    dec_term = dot_nn(lat_t[layers], whole_ct).astype(BF16)
    d_out[...] = dec_term.reshape(n, dec_rows, dec_term.shape[1])
    start(DEC_TERM)

    half = n // 2
    for layer in reversed(range(layers)):
        for lo, size in spans:
            product = car[lo : lo + size, :].astype(F32) * slope[layer, lo : lo + size, :]
            dpre[lo // block : (lo + size) // block] = product.astype(BF16).reshape(
                size // block, block, width
            )
        top = dot_nn(lat_t[layer], dpre[0:n].reshape(tokens, width)).astype(BF16)
        low = dot_nn(lat_t[layer], early_dpre(layer, 0, tokens)).astype(BF16)
        for j in range(n):
            piece = top if j < half else low
            first = (j % half) * own
            core_out[layer, j % 2, (j // 2) % 2, j // 4] = piece[first : first + own]
        send_core(layer)
        if layer + 1 < layers:
            send_y(layer + 1)
        if layer + 2 < layers:
            send_z(layer + 2)
        for lo, size in spans:
            same = dpre[lo // block : (lo + size) // block].reshape(size, width)
            back = dot_nt(same, temp_w[layer, 0:width, :])
            back = back + dot_nt(early_dpre(layer, lo, size), temp_w[layer, width:, :])
            car[lo : lo + size, :] = (car[lo : lo + size, :].astype(F32) + back).astype(BF16)
    send_y(0)
    send_z(1)

    enc_term = dot_nn(px_t[...], car[...])
    enc_term = enc_term.reshape(n, enc_term.shape[0] // n, width)
    lanes = e_out.shape[2]
    enc_term = jnp.concatenate(
        [enc_term[:, :, i : i + lanes] for i in range(0, width, lanes)], axis=1
    )
    e_out[...] = enc_term.astype(BF16)
    start(ENC_TERM)
    send_z(0)

    arrive(DEC_TERM)
    total = d_out[me].astype(F32)
    for k in range(1, n):
        total = total + d_in[k].astype(F32)
    grad_dec[...] = total
    for layer in range(layers - 1, 0, -1):
        finish(layer)
    arrive(DECODE)
    arrive(ENC_TERM)
    total = e_out[me].astype(F32)
    for k in range(1, n):
        total = total + e_in[k].astype(F32)
    enc_rows = grad_enc.shape[0]
    for i in range(width // lanes):
        grad_enc[:, i * lanes : (i + 1) * lanes] = total[i * enc_rows : (i + 1) * enc_rows]
    for kind in range(ENC_TERM + 1):
        sent(kind)
    finish(0)


def kernel_shards(
    n, patches, classes, dilations, enc_weight, cond_table, temp_weight, dec_weight, cotangent
):
    _, pixels, features = patches.shape
    layers, deep, width = temp_weight.shape
    block = pixels // n
    margin = n // 4
    tokens = n * block
    own = deep // n
    lanes = features
    nz = n // 4
    hbm = pl.BlockSpec(memory_space=pltpu.HBM)
    kinds = cond_table.shape[0]
    small = width // n
    vmem = pl.BlockSpec(memory_space=pltpu.VMEM)
    smem = pl.BlockSpec(memory_space=pltpu.SMEM)
    chunk = tokens // 2
    decoded, grad_enc, grad_temp, grad_dec = pl.pallas_call(
        functools.partial(step_kernel, n, layers, margin, chunk),
        out_shape=(
            jax.ShapeDtypeStruct((n, block, features), BF16),
            jax.ShapeDtypeStruct((features // n, width), F32),
            jax.ShapeDtypeStruct((layers, own, width), F32),
            jax.ShapeDtypeStruct((width // n, features), F32),
        ),
        in_specs=[smem, smem] + [hbm] * 6,
        out_specs=(vmem,) * 4,
        scratch_shapes=[
            pltpu.VMEM((features, width), BF16),
            pltpu.VMEM((kinds, width), BF16),
            pltpu.VMEM((layers, deep, width), BF16),
            pltpu.VMEM((width, features), BF16),
            pltpu.VMEM((kinds, 1, width), F32),
            pltpu.VMEM((n, block, features), BF16),
            pltpu.VMEM((n, block, features), BF16),
            pltpu.VMEM((n, 1, width), F32),
            pltpu.VMEM((layers + 1, margin + n, block, width), BF16),
            pltpu.VMEM((layers, tokens, width), F32),
            pltpu.VMEM((layers + 1, width, tokens), BF16),
            pltpu.VMEM((features, tokens), BF16),
            pltpu.VMEM((n + margin, block, width), BF16),
            pltpu.VMEM((tokens, width), BF16),
            pltpu.VMEM((n, block, features), BF16),
            pltpu.VMEM((layers, 2, 2, nz, own, width), BF16),
            pltpu.VMEM((layers, 2, nz, own, width), BF16),
            pltpu.VMEM((layers, nz, own, width), BF16),
            pltpu.VMEM((layers, nz, own, width), BF16),
            pltpu.VMEM((layers, nz, own, width), BF16),
            pltpu.VMEM((layers, nz, own, width), BF16),
            pltpu.VMEM((n, small, lanes), BF16),
            pltpu.VMEM((n, small, lanes), BF16),
            pltpu.VMEM((n, small, lanes), BF16),
            pltpu.VMEM((n, small, lanes), BF16),
            pltpu.SemaphoreType.DMA((6,)),
            pltpu.SemaphoreType.DMA((ENC_TERM + 1, n)),
            pltpu.SemaphoreType.DMA((ENC_TERM + 1, n)),
            pltpu.SemaphoreType.DMA((layers, nz + 1)),
            pltpu.SemaphoreType.DMA((layers, nz + 1)),
        ],
        compiler_params=pltpu.CompilerParams(
            collective_id=0, has_side_effects=True, vmem_limit_bytes=48 * 1024 * 1024
        ),
    )(
        dilations, classes, patches.reshape(n, block, features), enc_weight, cond_table,
        temp_weight, dec_weight, cotangent.reshape(n, block, features),
    )
    return decoded.reshape(1, pixels, features), grad_enc, grad_temp, grad_dec


def shift_late(values, spacing, margin):
    filler = jnp.zeros((margin,) + values.shape[1:], values.dtype)
    padded = jnp.concatenate([filler, values], axis=0)
    return lax.dynamic_slice_in_dim(padded, margin - spacing, values.shape[0], 0)


def shift_early(values, spacing, margin):
    filler = jnp.zeros((margin,) + values.shape[1:], values.dtype)
    padded = jnp.concatenate([values, filler], axis=0)
    return lax.dynamic_slice_in_dim(padded, spacing, values.shape[0], 0)


def plain_shards(
    patches, classes, dilations, enc_weight, cond_table, temp_weight, dec_weight, cotangent
):
    layers, _, width = temp_weight.shape
    block_patches = lax.all_to_all(patches, "tm", split_axis=1, concat_axis=0, tiled=True)
    block_cot = lax.all_to_all(cotangent, "tm", split_axis=1, concat_axis=0, tiled=True)
    frame_kinds = lax.all_gather(classes, "tm", tiled=True)
    kinds = cond_table.shape[0]
    onehot = (frame_kinds[:, None] == jnp.arange(kinds, dtype=jnp.int32)[None, :]).astype(BF16)
    embedded = jnp.dot(onehot, cond_table, preferred_element_type=F32)
    begin = jnp.einsum("tpc,cd->tpd", block_patches, enc_weight, preferred_element_type=F32)
    latent = (begin + embedded[:, None, :]).astype(BF16)
    margin = latent.shape[0] // 4
    saved = []
    for layer in range(layers):
        joined = jnp.concatenate([latent, shift_late(latent, dilations[layer], margin)], axis=-1)
        pre = jnp.einsum("tpk,kd->tpd", joined, temp_weight[layer], preferred_element_type=F32)
        saved.append((joined, pre))
        latent = (latent.astype(F32) + jax.nn.silu(pre)).astype(BF16)
    block_out = jnp.einsum(
        "tpd,dc->tpc", latent, dec_weight, preferred_element_type=F32
    ).astype(BF16)
    decoded = lax.all_to_all(block_out, "tm", split_axis=0, concat_axis=1, tiled=True)
    dec_term = jnp.einsum("tpd,tpc->dc", latent, block_cot, preferred_element_type=F32)
    carried = jnp.einsum(
        "tpc,dc->tpd", block_cot, dec_weight, preferred_element_type=F32
    ).astype(BF16)
    terms = [None] * layers
    for layer in reversed(range(layers)):
        joined, pre = saved[layer]
        s = jax.nn.sigmoid(pre)
        dpre = (carried.astype(F32) * s * (1.0 + pre * (1.0 - s))).astype(BF16)
        terms[layer] = jnp.einsum("tpk,tpd->kd", joined, dpre, preferred_element_type=F32)
        back = jnp.einsum("tpd,kd->tpk", dpre, temp_weight[layer], preferred_element_type=F32)
        carried = (
            carried.astype(F32)
            + back[..., :width]
            + shift_early(back[..., width:], dilations[layer], margin)
        ).astype(BF16)
    enc_term = jnp.einsum("tpc,tpd->cd", block_patches, carried, preferred_element_type=F32)
    return (
        decoded,
        lax.psum_scatter(enc_term, "tm", scatter_dimension=0, tiled=True),
        lax.psum_scatter(jnp.stack(terms), "tm", scatter_dimension=1, tiled=True),
        lax.psum_scatter(dec_term, "tm", scatter_dimension=0, tiled=True),
    )


def solution(mesh):
    n = mesh.shape["tm"]

    def shards(patches, *rest):
        pixels = patches.shape[1]
        deep, width = rest[4].shape[1:]
        whole = n % 4 == 0 and n >= 8 and pixels % n == 0 and (pixels // n) % 16 == 0 and (deep // n) % 16 == 0
        if whole and patches.shape[0] == 1 and (width // n) % 16 == 0:
            return kernel_shards(n, patches, *rest)
        return plain_shards(patches, *rest)

    in_specs = (
        P(("group", "tm"), None, None),
        P(("group", "tm")),
        P(),
        P(),
        P(),
        P(),
        P(),
        P(("group", "tm"), None, None),
    )
    out_specs = (
        P(("group", "tm"), None, None),
        P(("group", "tm"), None),
        P("group", "tm", None),
        P(("group", "tm"), None),
    )
    return jax.shard_map(shards, mesh=mesh, in_specs=in_specs, out_specs=out_specs, check_vma=False)
```

```python
import functools

import jax
import jax.numpy as jnp
from jax import lax
from jax.experimental import pallas as pl
from jax.experimental.pallas import tpu as pltpu
from jax.sharding import PartitionSpec as P

MESH = pl.DeviceIdType.MESH
F32 = jnp.float32
BF16 = jnp.bfloat16

PATCH, EMBED, COTAN, DECODE, DEC_TERM, ENC_TERM = range(6)


def dot_nt(a, b):
    return lax.dot_general(a, b, (((1,), (1,)), ((), ())), preferred_element_type=F32)


def dot_nn(a, b):
    return jnp.dot(a, b, preferred_element_type=F32)


def step_kernel(
    n, layers, margin, chunk,
    dil, cls, patches, enc_hbm, cond_hbm, temp_hbm, dec_hbm, cot,
    decoded, grad_enc, grad_temp, grad_dec,
    enc_w, cond, temp_w, dec_w, cond_rows,
    px, ct, emb, lat, slope, lat_t, px_t, dpre, car, dec_send,
    core_out, core_in, y_out, y_in, z_out, z_in, d_out, d_in, e_out, e_in,
    local_sem, send_sem, recv_sem, stage_send, stage_recv,
):
    me = lax.axis_index("tm")
    core = lax.rem(me, 2)
    y = lax.rem(lax.div(me, 2), 2)
    z = lax.div(me, 4)
    nz = n // 4
    block = px.shape[1]
    tokens = n * block
    width = enc_w.shape[1]
    own = core_out.shape[4]

    local = [
        pltpu.make_async_copy(src, dst, local_sem.at[i])
        for i, (src, dst) in enumerate(
            [
                (cond_hbm, cond),
                (patches.at[me], px.at[me]),
                (enc_hbm, enc_w),
                (temp_hbm, temp_w),
                (dec_hbm, dec_w),
                (cot.at[me], ct.at[me]),
            ]
        )
    ]
    for fetch in local:
        fetch.start()

    def copy(kind, k, src, dst):
        return pltpu.make_async_remote_copy(
            src_ref=src,
            dst_ref=dst,
            send_sem=send_sem.at[kind],
            recv_sem=recv_sem.at[kind],
            device_id={"tm": lax.rem(me + k, n)},
            device_id_type=MESH,
        )

    def descriptor(kind, k):
        peer = lax.rem(me + k, n)
        if kind == PATCH:
            return copy(kind, k, patches.at[peer], px.at[me])
        if kind == EMBED:
            return copy(kind, k, emb.at[me], emb.at[me])
        if kind == COTAN:
            return copy(kind, k, cot.at[peer], ct.at[me])
        if kind == DECODE:
            return copy(kind, k, dec_send.at[peer], decoded.at[me])
        if kind == DEC_TERM:
            return copy(kind, k, d_out.at[peer], d_in.at[k])
        return copy(kind, k, e_out.at[peer], e_in.at[k])

    def everything(kind):
        landed = [px, emb, ct, decoded, d_in, e_in][kind].at[pl.ds(1, n - 1)]
        return copy(kind, 1, landed, landed)

    def each(fn):
        lax.fori_loop(1, n, lambda k, c: (fn(k), c)[1], 0)

    def start(kind):
        each(lambda k: descriptor(kind, k).start())

    def arrive(kind):
        everything(kind).wait_recv()

    def sent(kind):
        everything(kind).wait_send()

    def staged(layer, stage, src, dst, peer):
        return pltpu.make_async_remote_copy(
            src_ref=src,
            dst_ref=dst,
            send_sem=stage_send.at[layer, stage],
            recv_sem=stage_recv.at[layer, stage],
            device_id={"tm": peer},
            device_id_type=MESH,
        )

    def core_copy(layer):
        return staged(
            layer, 0, core_out.at[layer, 1 - core], core_in.at[layer], me + 1 - 2 * core
        )

    def y_copy(layer):
        return staged(layer, 1, y_out.at[layer], y_in.at[layer], me + 2 - 4 * y)

    def z_copy(layer, k):
        there = lax.rem(z + k, nz)
        peer = there * 4 + y * 2 + core
        return staged(layer, 1 + k, z_out.at[layer, there], z_in.at[layer, k], peer)

    def send_core(layer):
        core_copy(layer).start()

    def send_y(layer):
        core_copy(layer).wait_recv()
        total = core_out[layer, core, 1 - y].astype(F32) + core_in[layer, 1 - y].astype(F32)
        y_out[layer] = total.astype(BF16)
        y_copy(layer).start()

    def send_z(layer):
        y_copy(layer).wait_recv()
        total = core_out[layer, core, y].astype(F32) + core_in[layer, y].astype(F32)
        z_out[layer] = (total + y_in[layer].astype(F32)).astype(BF16)
        for k in range(1, nz):
            z_copy(layer, k).start()

    def finish(layer):
        total = z_out[layer, z].astype(F32)
        for k in range(1, nz):
            z_copy(layer, k).wait_recv()
            total = total + z_in[layer, k].astype(F32)
        grad_temp[layer] = total
        core_copy(layer).wait_send()
        y_copy(layer).wait_send()
        for k in range(1, nz):
            z_copy(layer, k).wait_send()

    barrier = pltpu.get_barrier_semaphore()
    each(
        lambda k: pl.semaphore_signal(
            barrier, inc=1, device_id={"tm": lax.rem(me + k, n)}, device_id_type=MESH
        )
    )
    local[0].wait()
    kinds = cond.shape[0]
    cond_rows[...] = cond[...].astype(F32).reshape(kinds, 1, width)
    emb[me] = cond_rows[cls[0]]
    pl.semaphore_wait(barrier, n - 1)
    start(EMBED)
    start(PATCH)
    start(COTAN)

    spans = [(c * chunk, chunk) for c in range(tokens // chunk)]

    def latents(layer, lo, size):
        first = margin + lo // block
        return lat[layer, first : first + size // block].reshape(size, width)

    def put_latents(layer, lo, value):
        first = margin + lo // block
        frames = value.shape[0] // block
        lat[layer, first : first + frames] = value.reshape(frames, block, width)

    def late_latents(layer, lo, size):
        back = margin - dil[layer] + lo // block
        return jnp.concatenate([lat[layer, back + i] for i in range(size // block)], axis=0)

    def early_dpre(layer, lo, size):
        ahead = dil[layer] + lo // block
        return jnp.concatenate([dpre[ahead + i] for i in range(size // block)], axis=0)

    for layer in range(layers):
        lat[layer, 0:margin] = jnp.zeros((margin, block, width), BF16)
    dpre[n : n + margin] = jnp.zeros((margin, block, width), BF16)

    for fetch in local[1:]:
        fetch.wait()
    arrive(PATCH)
    arrive(EMBED)

    for lo, size in spans:
        frames = size // block
        first = lo // block
        rows = px[first : first + frames].reshape(size, px.shape[2])
        begin = dot_nn(rows, enc_w[...]).reshape(frames, block, width)
        begin = begin + emb[first : first + frames]
        put_latents(0, lo, begin.reshape(size, width).astype(BF16))
        px_t[:, lo : lo + size] = rows.T

    for layer in range(layers):
        for lo, size in spans:
            now = latents(layer, lo, size)
            late = late_latents(layer, lo, size)
            pre = dot_nn(now, temp_w[layer, 0:width, :]) + dot_nn(late, temp_w[layer, width:, :])
            s = 0.5 + 0.5 * jnp.tanh(0.5 * pre)
            act = pre * s
            put_latents(layer + 1, lo, (now.astype(F32) + act).astype(BF16))
            slope[layer, lo : lo + size, :] = s + act * (1.0 - s)
            lat_t[layer, :, lo : lo + size] = now.T

    for lo, size in spans:
        now = latents(layers, lo, size)
        out = dot_nn(now, dec_w[...]).astype(BF16)
        dec_send[lo // block : (lo + size) // block] = out.reshape(size // block, block, out.shape[1])
        lat_t[layers, :, lo : lo + size] = now.T
    start(DECODE)
    decoded[me] = dec_send[me]
    arrive(COTAN)

    for lo, size in spans:
        rows = ct[lo // block : (lo + size) // block].reshape(size, ct.shape[2])
        car[lo : lo + size, :] = dot_nt(rows, dec_w[...]).astype(BF16)

    dec_rows = d_out.shape[1]
    whole_ct = ct[...].reshape(tokens, ct.shape[2])
    dec_term = dot_nn(lat_t[layers], whole_ct).astype(BF16)
    d_out[...] = dec_term.reshape(n, dec_rows, dec_term.shape[1])
    start(DEC_TERM)

    half = n // 2
    for layer in reversed(range(layers)):
        for lo, size in spans:
            product = car[lo : lo + size, :].astype(F32) * slope[layer, lo : lo + size, :]
            dpre[lo // block : (lo + size) // block] = product.astype(BF16).reshape(
                size // block, block, width
            )
        top = dot_nn(lat_t[layer], dpre[0:n].reshape(tokens, width)).astype(BF16)
        low = dot_nn(lat_t[layer], early_dpre(layer, 0, tokens)).astype(BF16)
        for j in range(n):
            piece = top if j < half else low
            first = (j % half) * own
            core_out[layer, j % 2, (j // 2) % 2, j // 4] = piece[first : first + own]
        send_core(layer)
        if layer + 1 < layers:
            send_y(layer + 1)
        if layer + 2 < layers:
            send_z(layer + 2)
        for lo, size in spans:
            same = dpre[lo // block : (lo + size) // block].reshape(size, width)
            back = dot_nt(same, temp_w[layer, 0:width, :])
            back = back + dot_nt(early_dpre(layer, lo, size), temp_w[layer, width:, :])
            car[lo : lo + size, :] = (car[lo : lo + size, :].astype(F32) + back).astype(BF16)
    send_y(0)
    send_z(1)

    enc_term = dot_nn(px_t[...], car[...])
    enc_term = enc_term.reshape(n, enc_term.shape[0] // n, width)
    lanes = e_out.shape[2]
    enc_term = jnp.concatenate(
        [enc_term[:, :, i : i + lanes] for i in range(0, width, lanes)], axis=1
    )
    e_out[...] = enc_term.astype(BF16)
    start(ENC_TERM)
    send_z(0)

    arrive(DEC_TERM)
    total = d_out[me].astype(F32)
    for k in range(1, n):
        total = total + d_in[k].astype(F32)
    grad_dec[...] = total
    for layer in range(layers - 1, 0, -1):
        finish(layer)
    arrive(DECODE)
    arrive(ENC_TERM)
    total = e_out[me].astype(F32)
    for k in range(1, n):
        total = total + e_in[k].astype(F32)
    enc_rows = grad_enc.shape[0]
    for i in range(width // lanes):
        grad_enc[:, i * lanes : (i + 1) * lanes] = total[i * enc_rows : (i + 1) * enc_rows]
    for kind in range(ENC_TERM + 1):
        sent(kind)
    finish(0)


def kernel_shards(
    n, patches, classes, dilations, enc_weight, cond_table, temp_weight, dec_weight, cotangent
):
    _, pixels, features = patches.shape
    layers, deep, width = temp_weight.shape
    block = pixels // n
    margin = n // 4
    tokens = n * block
    own = deep // n
    lanes = features
    nz = n // 4
    hbm = pl.BlockSpec(memory_space=pltpu.HBM)
    kinds = cond_table.shape[0]
    small = width // n
    vmem = pl.BlockSpec(memory_space=pltpu.VMEM)
    smem = pl.BlockSpec(memory_space=pltpu.SMEM)
    chunk = tokens // 2
    decoded, grad_enc, grad_temp, grad_dec = pl.pallas_call(
        functools.partial(step_kernel, n, layers, margin, chunk),
        out_shape=(
            jax.ShapeDtypeStruct((n, block, features), BF16),
            jax.ShapeDtypeStruct((features // n, width), F32),
            jax.ShapeDtypeStruct((layers, own, width), F32),
            jax.ShapeDtypeStruct((width // n, features), F32),
        ),
        in_specs=[smem, smem] + [hbm] * 6,
        out_specs=(vmem,) * 4,
        scratch_shapes=[
            pltpu.VMEM((features, width), BF16),
            pltpu.VMEM((kinds, width), BF16),
            pltpu.VMEM((layers, deep, width), BF16),
            pltpu.VMEM((width, features), BF16),
            pltpu.VMEM((kinds, 1, width), F32),
            pltpu.VMEM((n, block, features), BF16),
            pltpu.VMEM((n, block, features), BF16),
            pltpu.VMEM((n, 1, width), F32),
            pltpu.VMEM((layers + 1, margin + n, block, width), BF16),
            pltpu.VMEM((layers, tokens, width), F32),
            pltpu.VMEM((layers + 1, width, tokens), BF16),
            pltpu.VMEM((features, tokens), BF16),
            pltpu.VMEM((n + margin, block, width), BF16),
            pltpu.VMEM((tokens, width), BF16),
            pltpu.VMEM((n, block, features), BF16),
            pltpu.VMEM((layers, 2, 2, nz, own, width), BF16),
            pltpu.VMEM((layers, 2, nz, own, width), BF16),
            pltpu.VMEM((layers, nz, own, width), BF16),
            pltpu.VMEM((layers, nz, own, width), BF16),
            pltpu.VMEM((layers, nz, own, width), BF16),
            pltpu.VMEM((layers, nz, own, width), BF16),
            pltpu.VMEM((n, small, lanes), BF16),
            pltpu.VMEM((n, small, lanes), BF16),
            pltpu.VMEM((n, small, lanes), BF16),
            pltpu.VMEM((n, small, lanes), BF16),
            pltpu.SemaphoreType.DMA((6,)),
            pltpu.SemaphoreType.DMA((ENC_TERM + 1,)),
            pltpu.SemaphoreType.DMA((ENC_TERM + 1,)),
            pltpu.SemaphoreType.DMA((layers, nz + 1)),
            pltpu.SemaphoreType.DMA((layers, nz + 1)),
        ],
        compiler_params=pltpu.CompilerParams(
            collective_id=0, has_side_effects=True, vmem_limit_bytes=60 * 1024 * 1024
        ),
    )(
        dilations, classes, patches.reshape(n, block, features), enc_weight, cond_table,
        temp_weight, dec_weight, cotangent.reshape(n, block, features),
    )
    return decoded.reshape(1, pixels, features), grad_enc, grad_temp, grad_dec


def shift_late(values, spacing, margin):
    filler = jnp.zeros((margin,) + values.shape[1:], values.dtype)
    padded = jnp.concatenate([filler, values], axis=0)
    return lax.dynamic_slice_in_dim(padded, margin - spacing, values.shape[0], 0)


def shift_early(values, spacing, margin):
    filler = jnp.zeros((margin,) + values.shape[1:], values.dtype)
    padded = jnp.concatenate([values, filler], axis=0)
    return lax.dynamic_slice_in_dim(padded, spacing, values.shape[0], 0)


def plain_shards(
    patches, classes, dilations, enc_weight, cond_table, temp_weight, dec_weight, cotangent
):
    layers, _, width = temp_weight.shape
    block_patches = lax.all_to_all(patches, "tm", split_axis=1, concat_axis=0, tiled=True)
    block_cot = lax.all_to_all(cotangent, "tm", split_axis=1, concat_axis=0, tiled=True)
    frame_kinds = lax.all_gather(classes, "tm", tiled=True)
    kinds = cond_table.shape[0]
    onehot = (frame_kinds[:, None] == jnp.arange(kinds, dtype=jnp.int32)[None, :]).astype(BF16)
    embedded = jnp.dot(onehot, cond_table, preferred_element_type=F32)
    begin = jnp.einsum("tpc,cd->tpd", block_patches, enc_weight, preferred_element_type=F32)
    latent = (begin + embedded[:, None, :]).astype(BF16)
    margin = latent.shape[0] // 4
    saved = []
    for layer in range(layers):
        joined = jnp.concatenate([latent, shift_late(latent, dilations[layer], margin)], axis=-1)
        pre = jnp.einsum("tpk,kd->tpd", joined, temp_weight[layer], preferred_element_type=F32)
        saved.append((joined, pre))
        latent = (latent.astype(F32) + jax.nn.silu(pre)).astype(BF16)
    block_out = jnp.einsum(
        "tpd,dc->tpc", latent, dec_weight, preferred_element_type=F32
    ).astype(BF16)
    decoded = lax.all_to_all(block_out, "tm", split_axis=0, concat_axis=1, tiled=True)
    dec_term = jnp.einsum("tpd,tpc->dc", latent, block_cot, preferred_element_type=F32)
    carried = jnp.einsum(
        "tpc,dc->tpd", block_cot, dec_weight, preferred_element_type=F32
    ).astype(BF16)
    terms = [None] * layers
    for layer in reversed(range(layers)):
        joined, pre = saved[layer]
        s = jax.nn.sigmoid(pre)
        dpre = (carried.astype(F32) * s * (1.0 + pre * (1.0 - s))).astype(BF16)
        terms[layer] = jnp.einsum("tpk,tpd->kd", joined, dpre, preferred_element_type=F32)
        back = jnp.einsum("tpd,kd->tpk", dpre, temp_weight[layer], preferred_element_type=F32)
        carried = (
            carried.astype(F32)
            + back[..., :width]
            + shift_early(back[..., width:], dilations[layer], margin)
        ).astype(BF16)
    enc_term = jnp.einsum("tpc,tpd->cd", block_patches, carried, preferred_element_type=F32)
    return (
        decoded,
        lax.psum_scatter(enc_term, "tm", scatter_dimension=0, tiled=True),
        lax.psum_scatter(jnp.stack(terms), "tm", scatter_dimension=1, tiled=True),
        lax.psum_scatter(dec_term, "tm", scatter_dimension=0, tiled=True),
    )


def solution(mesh):
    n = mesh.shape["tm"]

    def shards(patches, *rest):
        pixels = patches.shape[1]
        deep, width = rest[4].shape[1:]
        whole = n % 4 == 0 and n >= 8 and pixels % n == 0 and (pixels // n) % 16 == 0 and (deep // n) % 16 == 0
        if whole and patches.shape[0] == 1 and (width // n) % 16 == 0:
            return kernel_shards(n, patches, *rest)
        return plain_shards(patches, *rest)

    in_specs = (
        P(("group", "tm"), None, None),
        P(("group", "tm")),
        P(),
        P(),
        P(),
        P(),
        P(),
        P(("group", "tm"), None, None),
    )
    out_specs = (
        P(("group", "tm"), None, None),
        P(("group", "tm"), None),
        P("group", "tm", None),
        P(("group", "tm"), None),
    )
    return jax.shard_map(shards, mesh=mesh, in_specs=in_specs, out_specs=out_specs, check_vma=False)
```
